256 devices in a mesh: expert: 16 (over x, z_lo), dp: 16 (over y, z_hi, core).
Axes of the slice: x: 4, y: 4, z: 8 (z_hi: 2, z_lo: 4; z = z_hi * 4 + z_lo), core: 2. Of those that a mesh axis runs over, the one named last changes fastest.
Arguments:
- tokens: bfloat16 [65536, 1024], P(('expert', 'dp')), may hold values from -6 to 6
- route_ids: int32 [65536, 2], P(('expert', 'dp')), may hold values from 0 to 15, all different within a row; in each aligned block of 256 rows (0 to 255, 256 to 511, ...) at most 48 rows name the same one
- gate_values: float32 [65536, 2], P(('expert', 'dp')), may hold values from 0.2 to 1
- w_gate: bfloat16 [16, 1024, 1024], P('expert', 'dp'), may hold values from -0.1875 to 0.1875
- w_up: bfloat16 [16, 1024, 1024], P('expert', 'dp'), may hold values from -0.1875 to 0.1875
- w_down: bfloat16 [16, 1024, 1024], P('expert', 'dp'), may hold values from -0.1875 to 0.1875
- swap_flags: int32 [16], replicated, may hold values from 0 to 1, as said below
- out_grad: bfloat16 [65536, 1024], P(('expert', 'dp')), may hold values from -6 to 6
Outputs:
- layer_out: bfloat16 [65536, 1024], P(('expert', 'dp'))
- grad_tokens: bfloat16 [65536, 1024], P(('expert', 'dp'))
- grad_gate: float32 [16, 1024, 1024], P('expert', 'dp')
- grad_up: float32 [16, 1024, 1024], P('expert', 'dp')
- grad_down: float32 [16, 1024, 1024], P('expert', 'dp')
The draws below stay inside these ranges and needn't reach their ends.
Inputs may be any that keep to these rules, and one draw needn't show every extreme that they name: `route_ids`: within the rows of one device (256 tokens) no expert is named by more than 48 token-expert pairs, a bound that some block reaches; a token's 2 experts differ. `swap_flags`: the first and the last pair always exchange their experts.
All inputs are finite; a program needn't handle non-finite values.
Results may differ from the reference program's by a relative error of at most 0.012.
Values may be sent and summed in bfloat16 or wider, within the bound.
No kernel may reach another device: no remote copies, remote signals or barrier semaphores. Data moves between devices by JAX's collectives and lax.ppermute only.
A program may use at most 64 MiB of HBM per device.

```python
import math
import jax
import jax.numpy as jnp
import numpy as np
from jax import lax

D = 1024
F = 1024
EXP_DEV = 1
TOP = 2
TOK_DEV = 256
EXPERTS = 16
CAP = 48
TOKENS = 65536
SWAP_PAIRS = 8
N_EXPERT = 16
N_DP = 16


def draw_swap_flags(key, part):
    flag_bits = jax.random.randint(key, (N_EXPERT,), 0, 2).astype(jnp.int32)
    flag_bits = flag_bits.at[0].set(1 - flag_bits[SWAP_PAIRS])
    flag_bits = flag_bits.at[SWAP_PAIRS - 1].set(1 - flag_bits[N_EXPERT - 1])
    return flag_bits.astype(jnp.int32)


def level_of(own_key, extent, pieces, smallest, top_value):
    level, own = 1.0, jax.random.fold_in(own_key, 6)
    for axis_at, parts in pieces:
        heights = jnp.exp(jax.random.uniform(jax.random.fold_in(own, axis_at), (parts,), jnp.float32, smallest / len(pieces), top_value / len(pieces)))
        level = level * jnp.repeat(heights, extent[axis_at] // parts).reshape([-1 if axis == axis_at else 1 for axis in range(len(extent))])
    return level


def deal_out(rng, own, number, rows, count, top, most, skew):
    sequence = jax.random.permutation(rng, count)
    packed, ordinary = load_shares(count, rows * top, most, skew, True), load_shares(count, rows * top, most, skew, False)
    places = jnp.arange(count)

    def named(tallies, turn):
        used = int((tallies > 0).sum())
        fixed = max(1, used // 4)
        shifted = fixed + (places - fixed + turn * (used - fixed)) % max(1, count - fixed)
        return jnp.zeros((count,), jnp.int32).at[sequence[jnp.where(places < fixed, places, shifted)]].set(jnp.asarray(tallies, jnp.int32))

    tallies = jnp.where(number % 4 == 0, named(packed, number // 4), named(ordinary, number - number // 4 - 1))
    mixed = jax.random.permutation(jax.random.fold_in(own, 3), count)
    source_of, sink = mixed[0:count // 2 * 2:2], mixed[1:count // 2 * 2:2]
    slack = jnp.minimum(tallies[source_of] - 1, most - tallies[sink]) // 2
    slack = jnp.where((source_of == sequence[0]) | (sink == sequence[0]) | (tallies[sink] == 0), 0, jnp.maximum(slack, 0))
    shifted = jax.random.randint(jax.random.fold_in(own, 4), (count // 2,), 0, 1 << 20) % (slack + 1)
    tallies = tallies.at[source_of].add(-shifted).at[sink].add(shifted)
    items = jnp.searchsorted(jnp.cumsum(tallies), jnp.arange(rows * top), side="right").astype(jnp.int32)
    listing = items.reshape(top, rows).T
    listing = listing[jax.random.permutation(jax.random.fold_in(own, 1), rows)]
    turn = jax.random.randint(jax.random.fold_in(own, 2), (rows, 1), 0, top)
    return jnp.take_along_axis(listing, (jnp.arange(top)[None, :] + turn) % top, axis=1)


def load_shares(count, total, most, skew, full):
    portions = [(1 << 20) // math.isqrt(standing ** skew) + 1 for standing in range(1, count + 1)]
    largest = most if full else min(most, max(-(-total // count), total * portions[0] // sum(portions)))
    least = 1 if total - largest >= count - 1 else 0
    holding, rest = [largest] + [least] * (count - 1), total - largest - least * (count - 1)
    while rest > 0:
        movable = [i for i in range(1, count) if holding[i] < largest] or [i for i in range(1, count) if holding[i] < most]
        pool, budget = sum([portions[i] for i in movable]), rest
        for i in movable:
            addition = min(most - holding[i], max(1, budget * portions[i] // pool), rest)
            holding[i] = holding[i] + addition
            rest = rest - addition
    return np.array(holding)


def centred(own_key, shape, width, limit, cuts=(), kind=jnp.bfloat16):
    gain = level_of(own_key, shape, cuts, -0.22, 0.18) if cuts else 1.0
    array = jax.random.normal(own_key, shape, jnp.float32) * width * gain
    return jnp.minimum(jnp.maximum(array, -limit), limit).astype(kind)


def setup_inputs(seed: int = 0) -> dict:
    keys = jax.random.split(jax.random.key(seed), 9)
    tokens = centred(keys[0], (TOKENS, D), 1.0, 6.0, ((0, 256),))
    route_ids_keys = jax.random.split(jax.random.fold_in(keys[1], 1), TOKENS // TOK_DEV)
    route_ids_turns = jax.random.permutation(jax.random.fold_in(keys[1], 3), TOKENS // TOK_DEV)
    route_ids = jax.vmap(lambda own, number: deal_out(jax.random.fold_in(keys[1], 2), own, number, TOK_DEV, EXPERTS, TOP, CAP, 1))(route_ids_keys, route_ids_turns).reshape((TOKENS, TOP))
    gate_values = jnp.clip(0.2 + 0.8 * jax.random.uniform(keys[2], (TOKENS, TOP), jnp.float32) ** level_of(keys[2], (TOKENS, TOP), ((0, 256),), -0.2, 0.2), 0.2, 1.0)
    w_gate = centred(keys[3], (EXPERTS, D, F), D ** -0.5, 0.1875, ((0, 16), (1, 16)))
    w_up = centred(keys[4], (EXPERTS, D, F), D ** -0.5, 0.1875, ((0, 16), (1, 16)))
    w_down = centred(keys[5], (EXPERTS, F, D), F ** -0.5, 0.1875, ((0, 16), (1, 16)))
    swap_flags = draw_swap_flags(jax.random.fold_in(keys[8], 71), 0)
    out_grad = centred(keys[7], (TOKENS, D), 1.0, 6.0, ((0, 256),))
    return {"tokens": tokens, "route_ids": route_ids, "gate_values": gate_values, "w_gate": w_gate, "w_up": w_up, "w_down": w_down, "swap_flags": swap_flags, "out_grad": out_grad}


def round_half(values):
    return lax.optimization_barrier(values.astype(jnp.bfloat16)).astype(jnp.float32)


def reference(tokens, route_ids, gate_values, w_gate, w_up, w_down, swap_flags, out_grad):
    blocks = N_EXPERT * N_DP
    experts = EXP_DEV * N_EXPERT
    copies = TOK_DEV * TOP
    route_rows = route_ids.reshape(blocks, copies)
    onehot = (route_rows[:, :, None] == jnp.arange(experts, dtype=jnp.int32)[None, None, :]).astype(jnp.int32)
    rank_of = jnp.sum(jnp.cumsum(onehot, axis=1) * onehot, axis=2) - 1
    block_ids = jnp.broadcast_to(jnp.arange(blocks, dtype=jnp.int32)[:, None], (blocks, copies))
    copy_ids = jnp.broadcast_to(jnp.arange(copies, dtype=jnp.int32)[None, :], (blocks, copies))
    slot_table = jnp.full((blocks, experts, CAP), -1, jnp.int32).at[block_ids, route_rows, rank_of].set(copy_ids)
    gate_rows = gate_values.reshape(blocks, copies).astype(jnp.float32)
    column_ids = jnp.arange(blocks, dtype=jnp.int32)[:, None]

    def one_expert(totals, expert):
        mixed_sum, token_sum = totals
        rows_of = slot_table[:, expert, :]
        is_live = rows_of >= 0
        copy_pick = jnp.maximum(rows_of, 0)
        token_pick = (column_ids * TOK_DEV + copy_pick // TOP).reshape(-1)
        gate_pick = jnp.where(is_live, gate_rows[column_ids, copy_pick], 0.0).reshape(-1, 1)
        live_col = is_live.reshape(-1, 1)
        token_in = jnp.where(live_col, tokens[token_pick].astype(jnp.float32), 0.0)
        cot_in = round_half(gate_pick * out_grad[token_pick].astype(jnp.float32))
        gate_w = w_gate[expert].astype(jnp.float32)
        up_w = w_up[expert].astype(jnp.float32)
        down_w = w_down[expert].astype(jnp.float32)
        pre_gate = jnp.dot(token_in, gate_w)
        pre_up = jnp.dot(token_in, up_w)
        hidden = round_half(jax.nn.silu(pre_gate) * pre_up)
        expert_out = round_half(jnp.dot(hidden, down_w))
        mixed_sum = mixed_sum.at[token_pick].add(gate_pick * expert_out)
        grad_h = jnp.dot(cot_in, down_w.T)
        sigmoid_a = jax.nn.sigmoid(pre_gate)
        grad_a = round_half(grad_h * pre_up * sigmoid_a * (1.0 + pre_gate * (1.0 - sigmoid_a)))
        grad_b = round_half(grad_h * pre_gate * sigmoid_a)
        copy_grad = round_half(jnp.dot(grad_a, gate_w.T) + jnp.dot(grad_b, up_w.T))
        token_sum = token_sum.at[token_pick].add(copy_grad)
        token_four = token_in.reshape(N_EXPERT, N_DP, CAP, D)
        hidden_four = hidden.reshape(N_EXPERT, N_DP, CAP, F)
        cot_four = cot_in.reshape(N_EXPERT, N_DP, CAP, D)
        part_gate = round_half(jnp.einsum('idcx,idcf->dxf', token_four, grad_a.reshape(N_EXPERT, N_DP, CAP, F)))
        part_up = round_half(jnp.einsum('idcx,idcf->dxf', token_four, grad_b.reshape(N_EXPERT, N_DP, CAP, F)))
        part_down = round_half(jnp.einsum('idcf,idcx->dfx', hidden_four, cot_four))
        return (mixed_sum, token_sum), (jnp.sum(part_gate, axis=0), jnp.sum(part_up, axis=0), jnp.sum(part_down, axis=0))

    start_sums = (jnp.zeros((TOKENS, D), jnp.float32), jnp.zeros((TOKENS, D), jnp.float32))
    (mixed_sum, token_sum), stacked = lax.scan(one_expert, start_sums, jnp.arange(experts, dtype=jnp.int32))
    expert_ids = jnp.arange(experts, dtype=jnp.int32)
    owner = expert_ids // EXP_DEV
    pair_of = owner % SWAP_PAIRS
    paired = swap_flags[pair_of] != swap_flags[pair_of + SWAP_PAIRS]
    holder = jnp.where(paired, (owner + SWAP_PAIRS) % N_EXPERT, owner)
    slot_of = (holder * EXP_DEV + expert_ids % EXP_DEV).astype(jnp.int32)
    return (mixed_sum.astype(jnp.bfloat16), token_sum.astype(jnp.bfloat16), stacked[0][slot_of], stacked[1][slot_of], stacked[2][slot_of])
```

```python
import jax
import jax.numpy as jnp
from jax import lax
from jax.experimental import pallas as pl
from jax.experimental.pallas import tpu as pltpu
from jax.sharding import Mesh, PartitionSpec as P

AXES = ("x", "z_lo", "y", "z_hi", "core")
SIZES = (4, 4, 4, 2, 2)
CAP = 48
BF16 = jnp.bfloat16
F32 = jnp.float32
VMEM = pl.BlockSpec(memory_space=pltpu.VMEM)
SMEM = pl.BlockSpec(memory_space=pltpu.SMEM)


def flat(x, zl, y, zh, c):
    return (((x * 4 + zl) * 4 + y) * 2 + zh) * 2 + c


def z_pairs(j, back):
    pairs = []
    for x in range(4):
        for zl in range(4):
            for y in range(4):
                for zh in range(2):
                    for c in range(2):
                        step = (0, 1, 2 if c == 0 else -2, -1)[j]
                        z = (zh * 4 + zl + step) % 8
                        here, there = flat(x, zl, y, zh, c), flat(x, z % 4, y, z // 4, c)
                        pairs.append((there, here) if back else (here, there))
    return pairs


def z_move(a, j, back=False):
    return a if j == 0 else lax.ppermute(a, AXES, z_pairs(j, back))


def y_move(a, step):
    return lax.ppermute(a, "y", [(i, (i + step) % 4) for i in range(4)])


def x_swap(a):
    return lax.ppermute(a, "x", [(i, i ^ 2) for i in range(4)])


def x_exchange(a):
    return lax.all_to_all(a, "x", split_axis=0, concat_axis=0, tiled=True)


def flip(a, axis):
    return lax.ppermute(a, axis, [(0, 1), (1, 0)])


def iota(shape, dim):
    return lax.broadcasted_iota(jnp.int32, shape, dim)


def shape(*dims, dtype=BF16):
    return jax.ShapeDtypeStruct(dims, dtype)


def call(body, outs, ins, scratch=(), vmem=24, flops=0, moved=2**20):
    return pl.pallas_call(
        body,
        out_shape=outs,
        in_specs=ins,
        scratch_shapes=scratch,
        compiler_params=pltpu.CompilerParams(vmem_limit_bytes=vmem * 2**20),
        cost_estimate=pl.CostEstimate(flops=flops, bytes_accessed=moved, transcendentals=0),
    )


def copies(arrays, outs, pieces):
    n = len(arrays)

    def body(*refs):
        for i, at, o, to in pieces:
            refs[n + o][to] = refs[i][at]

    return pl.pallas_call(
        body,
        out_shape=tuple(outs),
        in_specs=[VMEM] * n,
        out_specs=tuple(VMEM for _ in outs),
        compiler_params=pltpu.CompilerParams(vmem_limit_bytes=16 * 2**20),
        cost_estimate=pl.CostEstimate(flops=0, bytes_accessed=4 * 2**20, transcendentals=0),
    )(*arrays)


ALL = slice(None)


def stack(arrays):
    return copies(
        arrays, [shape(len(arrays), *arrays[0].shape)], [(i, ALL, 0, i) for i in range(len(arrays))]
    )[0]


def join_classes(arrays):
    d = arrays[0].shape[-1]
    return copies(arrays, [shape(4, 4, CAP, d)], [(j, ALL, 0, (ALL, j)) for j in range(4)])[0]


def split_classes(a):
    d = a.shape[-1]
    return copies((a,), [shape(4, CAP, d)] * 4, [(0, (ALL, j), j, ALL) for j in range(4)])


def prep_kernel(place, flags, ids_ref, gate_ref, tok_ref, grad_ref, x0, x1, x2, x3, c_ref, slot_ref):
    t = ids_ref.shape[0]
    zl = place[3]
    ids = ids_ref[...]
    shift = jnp.zeros_like(ids)
    for p in range(8):
        step = jnp.where(flags[p] != flags[p + 8], 8, 0)
        shift = shift + jnp.where((ids & 7) == p, step, 0)
    holder = (ids + shift) & 15
    hx, hj = holder >> 2, ((holder & 3) - zl) & 3
    lab = hj * 4 + hx
    hot = [lab[:, k : k + 1] == iota((t, 16), 1) for k in range(2)]
    both = jnp.where(hot[0] | hot[1], 1.0, 0.0).astype(BF16)
    earlier = jnp.where(iota((t, t), 1) < iota((t, t), 0), 1.0, 0.0).astype(BF16)
    count = jnp.dot(earlier, both, preferred_element_type=F32)
    diagonal = iota((t, t), 0) == iota((t, t), 1)
    gate = gate_ref[...]
    slot, weight = [], []
    for k in range(2):
        rank = jnp.sum(jnp.where(hot[k], count, 0.0), axis=1, keepdims=True).astype(jnp.int32)
        col = lab[:, k : k + 1] * CAP + rank
        slot_ref[:, k : k + 1] = col
        slot_ref[:, k + 2 : k + 3] = (hx[:, k : k + 1] * 4 + hj[:, k : k + 1]) * CAP + rank
        slot.append(
            jnp.sum(jnp.where(diagonal, col.astype(F32), 0.0), axis=0, keepdims=True).astype(jnp.int32)
        )
        weight.append(jnp.sum(jnp.where(diagonal, gate[:, k : k + 1], 0.0), axis=0, keepdims=True))
    tok = tok_ref[...]
    grad = grad_ref[...]
    for j, out in enumerate((x0, x1, x2, x3)):
        rows = iota((4 * CAP, t), 0) + j * 4 * CAP
        m0, m1 = rows == slot[0], rows == slot[1]
        pick = jnp.where(m0 | m1, 1.0, 0.0).astype(BF16)
        scale = jnp.sum(
            jnp.where(m0, weight[0], 0.0) + jnp.where(m1, weight[1], 0.0), axis=1, keepdims=True
        )
        xr = jnp.dot(pick, tok, preferred_element_type=F32).astype(BF16)
        cr = (scale * jnp.dot(pick, grad, preferred_element_type=F32)).astype(BF16)
        for e in range(4):
            out[e] = xr[e * CAP : (e + 1) * CAP]
            c_ref[e, j] = cr[e * CAP : (e + 1) * CAP]


def mix_kernel(slot_ref, gate_ref, rows_ref, out_ref):
    gate = gate_ref[...]
    t, s = gate.shape[0], rows_ref.shape[0]
    rows = rows_ref[...]
    total = None
    for k in range(2):
        pick = jnp.where(iota((t, s), 1) == slot_ref[:, k + 2 : k + 3], 1.0, 0.0).astype(BF16)
        part = gate[:, k : k + 1] * jnp.dot(pick, rows, preferred_element_type=F32)
        total = part if total is None else total + part
    out_ref[...] = total.astype(BF16)


def add_kernel(slot_ref, r0, r1, r2, r3, out_ref):
    t = slot_ref.shape[0]
    total = None
    for j, ref in enumerate((r0, r1, r2, r3)):
        at = iota((t, 4 * CAP), 1) + j * 4 * CAP
        pick = jnp.where((at == slot_ref[:, 0:1]) | (at == slot_ref[:, 1:2]), 1.0, 0.0).astype(BF16)
        part = jnp.dot(pick, ref[...], preferred_element_type=F32)
        total = part if total is None else total + part
    out_ref[...] = total.astype(BF16)


def dot(a, b, ca, cb):
    return lax.dot_general(a, b, (((ca,), (cb,)), ((), ())), preferred_element_type=F32)


def expert_kernel(place, x_ref, c0, c1, c2, c3, near, near2, far, far2,
                  o0, o1, o2, o3, cg, mine, other, w, xs, cs, hid, ga, gb):
    y, zh, core = place[0], place[1], place[2]
    d = xs.shape[1]
    for m in range(3):
        for side, (n, f) in enumerate(((near, far), (near2, far2))):
            c = lax.rem(core + side, 2)
            for k, step in enumerate((0, 3, 1)):
                for h in range(2):
                    at = ((lax.rem(y + step, 4) * 2 + lax.rem(zh + h, 2)) * 2 + c) * 64
                    w[m, pl.ds(pl.multiple_of(at, 64), 64), :] = n[2 * k + h, m]
            for h in range(2):
                at = ((lax.rem(y + 2, 4) * 2 + lax.rem(zh + h, 2)) * 2 + c) * 64
                for q in range(2):
                    to = pl.multiple_of(at + 32 * q, 32)
                    w[m, pl.ds(to, 32), :] = f[q, m, 32 * h : 32 * h + 32]
    for j, c in enumerate((c0, c1, c2, c3)):
        for s in range(4):
            at = (j * 4 + s) * CAP
            xs[at : at + CAP] = x_ref[s, j]
            cs[at : at + CAP] = c[s]

    def first(n, _):
        cols = pl.ds(pl.multiple_of(n * 256, 256), 256)
        for r in range(3):
            rows = slice(r * 256, r * 256 + 256)
            pre_gate = dot(xs[rows], w[0, :, cols], 1, 0)
            pre_up = dot(xs[rows], w[1, :, cols], 1, 0)
            grad_h = dot(cs[rows], w[2, cols, :], 1, 1)
            sig = jax.nn.sigmoid(pre_gate)
            act = pre_gate * sig
            hid[rows, cols] = (act * pre_up).astype(BF16)
            ga[rows, cols] = (grad_h * pre_up * sig * (1.0 + pre_gate * (1.0 - sig))).astype(BF16)
            gb[rows, cols] = (grad_h * act).astype(BF16)
        return 0

    lax.fori_loop(0, 4, first, 0)

    def weight_grads(n, _):
        cols = pl.ds(pl.multiple_of(n * 256, 256), 256)
        rel = lax.rem(n + 4 - y, 4)
        for m, (left, right) in enumerate(((xs, ga), (xs, gb), (hid, cs))):
            part = dot(left[:, cols], right[...], 0, 0).astype(BF16)
            for h in range(2):
                p0, p1 = part[h * 128 : h * 128 + 64], part[h * 128 + 64 : h * 128 + 128]
                mine[rel, m, h] = jnp.where(core == 0, p0, p1)
                other[rel, m, h] = jnp.where(core == 0, p1, p0)
        return 0

    lax.fori_loop(0, 4, weight_grads, 0)

    def returns(n, _):
        cols = pl.ds(pl.multiple_of(n * 256, 256), 256)
        for j, o in enumerate((o0, o1, o2, o3)):
            rows = slice(j * 4 * CAP, (j + 1) * 4 * CAP)
            out = dot(hid[rows], w[2, :, cols], 1, 0).astype(BF16)
            back = (dot(ga[rows], w[0, cols, :], 1, 1) + dot(gb[rows], w[1, cols, :], 1, 1)).astype(BF16)
            for s in range(4):
                o[s, :, cols] = out[s * CAP : (s + 1) * CAP]
                cg[s, j, :, cols] = back[s * CAP : (s + 1) * CAP]
        return 0

    lax.fori_loop(0, 4, returns, 0)


def plus(a, b):
    return a.astype(F32) + b.astype(F32)


def far_kernel(mine, came, to_r, to_l):
    to_r[...] = plus(mine[2, :, :, 0:32], came[2, :, :, 0:32]).astype(BF16)
    to_l[...] = plus(mine[2, :, :, 32:64], came[2, :, :, 32:64]).astype(BF16)


def side_kernel(mine, came, fr, fl, to_r, to_l):
    lo, hi = slice(0, 32), slice(32, 64)
    to_r[:, :, lo] = (plus(mine[1, :, :, lo], came[1, :, :, lo]) + fr[...].astype(F32)).astype(BF16)
    to_r[:, :, hi] = plus(mine[1, :, :, hi], came[1, :, :, hi]).astype(BF16)
    to_l[:, :, lo] = plus(mine[3, :, :, lo], came[3, :, :, lo]).astype(BF16)
    to_l[:, :, hi] = (plus(mine[3, :, :, hi], came[3, :, :, hi]) + fl[...].astype(F32)).astype(BF16)


def here_kernel(place, mine, came, fr, fl, away, here):
    zh = place[1]
    for z, out in ((zh, here), (1 - zh, away)):
        total = plus(mine[0, :, z], came[0, :, z]) + plus(fr[:, z], fl[:, z])
        out[...] = total.astype(out.dtype)


def last_kernel(here, came, a, b, c):
    for m, out in enumerate((a, b, c)):
        out[0] = here[m] + came[m].astype(F32)


def shards(tokens, route_ids, gate_values, w_gate, w_up, w_down, swap_flags, out_grad):
    xi, zl = lax.axis_index("x"), lax.axis_index("z_lo")
    yi, zh, core = lax.axis_index("y"), lax.axis_index("z_hi"), lax.axis_index("core")
    t, d = tokens.shape
    own = xi * 4 + zl
    moved = swap_flags[own % 8] != swap_flags[own % 8 + 8]
    place = jnp.stack([yi, zh, core, zl]).astype(jnp.int32)
    flags = swap_flags.astype(jnp.int32)
    piece = shape(4, CAP, d)

    w_own = stack((w_gate[0], w_up[0], w_down[0]))
    w = jnp.where(moved, x_swap(w_own), w_own)
    *sent_x, sent_c, slot = call(
        prep_kernel,
        (piece, piece, piece, piece, shape(4, 4, CAP, d), shape(t, 4, dtype=jnp.int32)),
        [SMEM, SMEM] + [VMEM] * 4,
        flops=4 * 16 * CAP * t * d,
        moved=4 * 2**20,
    )(place, flags, route_ids, gate_values, tokens, out_grad)
    w, sent_x, sent_c = lax.optimization_barrier((w, sent_x, sent_c))
    w2 = flip(w, "z_hi")
    r0, l0 = y_move(w, 1), y_move(w, 3)

    came_x = [z_move(sent_x[j], j) for j in range(4)]
    came_c = x_exchange(sent_c)
    w2, came_x = lax.optimization_barrier((w2, came_x))
    r1, l1 = y_move(w2, 1), y_move(w2, 3)

    recv_x = x_exchange(join_classes(came_x))
    recv_c = [z_move(a, j) for j, a in enumerate(split_classes(came_c))]
    half = shape(3, 64, d)
    lo, hi = (ALL, slice(0, 32)), (ALL, slice(32, 64))
    near, to_r, to_l = copies(
        (w, w2, r0, r1, l0, l1),
        [shape(6, 3, 64, d), half, half],
        [(i, ALL, 0, i) for i in range(6)] + [(2, lo, 1, lo), (3, lo, 1, hi), (4, hi, 2, lo), (5, hi, 2, hi)],
    )
    fr, fl = y_move(to_r, 1), y_move(to_l, 3)
    near2 = flip(near, "core")
    far = stack((fr, fl))
    far2 = flip(far, "core")

    bf = lambda *dims: pltpu.VMEM(dims, BF16)
    *out, copy_grad, mine, other = call(
        expert_kernel,
        (piece, piece, piece, piece, shape(4, 4, CAP, d), shape(4, 3, 2, 64, d), shape(4, 3, 2, 64, d)),
        [SMEM] + [VMEM] * 9,
        [bf(3, d, d)] + [bf(16 * CAP, d) for _ in range(5)],
        vmem=52,
        flops=18 * 16 * CAP * d * d,
        moved=20 * 2**20,
    )(place, recv_x, *recv_c, near, near2, far, far2)

    out = [z_move(out[j], j, True) for j in range(4)]
    ret = x_exchange(copy_grad)
    came = flip(other, "core")
    piece3, row3 = shape(3, 2, 64, d), shape(3, 2, 32, d)
    to_r, to_l = call(far_kernel, (row3, row3), [VMEM] * 2)(mine, came)
    fr, fl = y_move(to_r, 1), y_move(to_l, 3)
    fr, fl, out = lax.optimization_barrier((fr, fl, out))
    to_r, to_l = call(side_kernel, (piece3, piece3), [VMEM] * 4)(mine, came, fr, fl)
    fr, fl = y_move(to_r, 1), y_move(to_l, 3)
    ret = [z_move(a, j, True).reshape(-1, d) for j, a in enumerate(split_classes(ret))]
    back = x_exchange(join_classes(out)).reshape(-1, d)
    fr, fl, ret = lax.optimization_barrier((fr, fl, ret))
    away, here = call(here_kernel, (shape(3, 64, d), shape(3, 64, d, dtype=F32)), [SMEM] + [VMEM] * 4)(
        place, mine, came, fr, fl
    )
    came = flip(away, "z_hi")
    layer_out = call(
        mix_kernel, shape(t, d), [VMEM] * 3, flops=4 * 16 * CAP * t * d, moved=2 * 2**20
    )(slot, gate_values, back)
    grad_tokens = call(
        add_kernel, shape(t, d), [VMEM] * 5, flops=2 * 16 * CAP * t * d, moved=2 * 2**20
    )(slot, *ret)
    one = shape(1, 64, d, dtype=F32)
    grads = call(last_kernel, (one, one, one), [VMEM] * 2)(here, came)
    return layer_out, grad_tokens, *grads


def solution(mesh):
    fine = Mesh(mesh.devices.reshape(SIZES), AXES)
    rows = P(AXES, None)
    weight = P(("x", "z_lo"), ("y", "z_hi", "core"), None)
    return jax.shard_map(
        shards,
        mesh=fine,
        in_specs=(rows, rows, rows, weight, weight, weight, P(), rows),
        out_specs=(rows, rows, weight, weight, weight),
        check_vma=False,
    )
```

```python
import jax
import jax.numpy as jnp
from jax import lax
from jax.experimental import pallas as pl
from jax.experimental.pallas import tpu as pltpu
from jax.sharding import Mesh, PartitionSpec as P

AXES = ("x", "z_lo", "y", "z_hi", "core")
SIZES = (4, 4, 4, 2, 2)
CAP = 48
BF16 = jnp.bfloat16
F32 = jnp.float32
HBM = pl.BlockSpec(memory_space=pltpu.HBM)
SMEM = pl.BlockSpec(memory_space=pltpu.SMEM)


def flat(x, zl, y, zh, c):
    return (((x * 4 + zl) * 4 + y) * 2 + zh) * 2 + c


def z_pairs(j, back):
    pairs = []
    for x in range(4):
        for zl in range(4):
            for y in range(4):
                for zh in range(2):
                    for c in range(2):
                        step = (0, 1, 2 if c == 0 else -2, -1)[j]
                        z = (zh * 4 + zl + step) % 8
                        here, there = flat(x, zl, y, zh, c), flat(x, z % 4, y, z // 4, c)
                        pairs.append((there, here) if back else (here, there))
    return pairs


def z_move(a, j, back=False):
    return a if j == 0 else lax.ppermute(a, AXES, z_pairs(j, back))


def y_move(a, step):
    return lax.ppermute(a, "y", [(i, (i + step) % 4) for i in range(4)])


def x_swap(a):
    return lax.ppermute(a, "x", [(i, i ^ 2) for i in range(4)])


def x_exchange(a):
    return lax.all_to_all(a, "x", split_axis=0, concat_axis=0, tiled=True)


def flip(a, axis):
    return lax.ppermute(a, axis, [(0, 1), (1, 0)])


def iota(shape, dim):
    return lax.broadcasted_iota(jnp.int32, shape, dim)


def shape(*dims, dtype=BF16):
    return jax.ShapeDtypeStruct(dims, dtype)


def staged(body, outs, arrays, smem=(), scratch=(), flops=0):
    k, n, m = len(smem), len(arrays), len(outs)
    part = [a[1] if isinstance(a, tuple) else None for a in arrays]
    arrays = [a[0] if isinstance(a, tuple) else a for a in arrays]

    def kernel(*refs):
        smems, srcs, dsts = refs[:k], refs[k : k + n], refs[k + n : k + n + m]
        ins, res = refs[k + n + m : k + 2 * n + m], refs[k + 2 * n + m : k + 2 * n + 2 * m]
        sems, rest = refs[-1], refs[k + 2 * n + 2 * m : -1]
        srcs = [a if i is None else a.at[i] for a, i in zip(srcs, part)]
        moves = [pltpu.make_async_copy(a, b, sems.at[i]) for i, (a, b) in enumerate(zip(srcs, ins))]
        for one in moves:
            one.start()
        for one in moves:
            one.wait()
        body(*smems, *ins, *res, *rest)
        moves = [pltpu.make_async_copy(a, b, sems.at[n + i]) for i, (a, b) in enumerate(zip(res, dsts))]
        for one in moves:
            one.start()
        for one in moves:
            one.wait()

    return pl.pallas_call(
        kernel,
        out_shape=tuple(outs),
        in_specs=[SMEM] * k + [HBM] * n,
        out_specs=tuple(HBM for _ in outs),
        scratch_shapes=[
            pltpu.VMEM(a.shape if i is None else a.shape[1:], a.dtype) for a, i in zip(arrays, part)
        ]
        + [pltpu.VMEM(o.shape, o.dtype) for o in outs]
        + list(scratch)
        + [pltpu.SemaphoreType.DMA((n + m,))],
        compiler_params=pltpu.CompilerParams(vmem_limit_bytes=60 * 2**20),
        cost_estimate=pl.CostEstimate(flops=flops, bytes_accessed=4 * 2**20, transcendentals=0),
    )(*smem, *arrays)


def copies(arrays, outs, pieces):
    n, m = len(arrays), len(outs)

    def kernel(*refs):
        srcs, dsts, mids, sems = refs[:n], refs[n : n + m], refs[n + m : n + 2 * m], refs[-1]
        moves = [
            pltpu.make_async_copy(srcs[i].at[at], mids[o].at[to], sems.at[p])
            for p, (i, at, o, to) in enumerate(pieces)
        ]
        for one in moves:
            one.start()
        for one in moves:
            one.wait()
        moves = [
            pltpu.make_async_copy(a, b, sems.at[len(pieces) + o]) for o, (a, b) in enumerate(zip(mids, dsts))
        ]
        for one in moves:
            one.start()
        for one in moves:
            one.wait()

    return pl.pallas_call(
        kernel,
        out_shape=tuple(outs),
        in_specs=[HBM] * n,
        out_specs=tuple(HBM for _ in outs),
        scratch_shapes=[pltpu.VMEM(o.shape, o.dtype) for o in outs]
        + [pltpu.SemaphoreType.DMA((len(pieces) + m,))],
        compiler_params=pltpu.CompilerParams(vmem_limit_bytes=60 * 2**20),
        cost_estimate=pl.CostEstimate(flops=0, bytes_accessed=4 * 2**20, transcendentals=0),
    )(*arrays)


ALL = slice(None)


def stack(arrays):
    return copies(
        arrays, [shape(len(arrays), *arrays[0].shape)], [(i, ALL, 0, i) for i in range(len(arrays))]
    )[0]


def join_classes(arrays):
    d = arrays[0].shape[-1]
    return copies(arrays, [shape(4, 4, CAP, d)], [(j, ALL, 0, (ALL, j)) for j in range(4)])[0]


def split_classes(a):
    d = a.shape[-1]
    return copies((a,), [shape(4, CAP, d)] * 4, [(0, (ALL, j), j, ALL) for j in range(4)])


def prep_kernel(flags, ids_ref, gate_ref, tok_ref, grad_ref, x0, x1, x2, x3, c_ref, slot_ref):
    t = ids_ref.shape[1]
    zl = lax.axis_index("z_lo")
    ids = ids_ref[...]
    shift = jnp.zeros_like(ids)
    for p in range(8):
        step = jnp.where(flags[p] != flags[p + 8], 8, 0)
        shift = shift + jnp.where((ids & 7) == p, step, 0)
    holder = (ids + shift) & 15
    hx, hj = holder >> 2, ((holder & 3) - zl) & 3
    lab = hj * 4 + hx
    hot = [lab[k : k + 1, :] == iota((16, t), 0) for k in range(2)]
    both = jnp.where(hot[0] | hot[1], 1.0, 0.0).astype(BF16)
    earlier = jnp.where(iota((t, t), 0) < iota((t, t), 1), 1.0, 0.0).astype(BF16)
    count = jnp.dot(both, earlier, preferred_element_type=F32)
    diagonal = iota((t, t), 0) == iota((t, t), 1)
    gate = gate_ref[...]
    slot, weight = [], []
    for k in range(2):
        rank = jnp.sum(jnp.where(hot[k], count, 0.0), axis=0, keepdims=True).astype(jnp.int32)
        one, two = lab[k : k + 1, :] * CAP + rank, (hx[k : k + 1, :] * 4 + hj[k : k + 1, :]) * CAP + rank
        slot.append(one)
        weight.append(gate[k : k + 1, :])
        for at, row in ((k, one.astype(F32)), (k + 2, two.astype(F32)), (k + 4, weight[k])):
            slot_ref[:, at : at + 1] = jnp.sum(jnp.where(diagonal, row, 0.0), axis=1, keepdims=True)
    tok = tok_ref[...]
    grad = grad_ref[...]
    for j, out in enumerate((x0, x1, x2, x3)):
        rows = iota((4 * CAP, t), 0) + j * 4 * CAP
        m0, m1 = rows == slot[0], rows == slot[1]
        pick = jnp.where(m0 | m1, 1.0, 0.0).astype(BF16)
        scale = jnp.sum(
            jnp.where(m0, weight[0], 0.0) + jnp.where(m1, weight[1], 0.0), axis=1, keepdims=True
        )
        xr = jnp.dot(pick, tok, preferred_element_type=F32).astype(BF16)
        cr = (scale * jnp.dot(pick, grad, preferred_element_type=F32)).astype(BF16)
        for e in range(4):
            out[e] = xr[e * CAP : (e + 1) * CAP]
            c_ref[e, j] = cr[e * CAP : (e + 1) * CAP]


def mix_kernel(slot_ref, rows_ref, out_ref):
    t, s = slot_ref.shape[0], rows_ref.shape[0]
    rows = rows_ref[...]
    total = None
    for k in range(2):
        slot = slot_ref[:, k + 2 : k + 3].astype(jnp.int32)
        pick = jnp.where(iota((t, s), 1) == slot, 1.0, 0.0).astype(BF16)
        part = slot_ref[:, k + 4 : k + 5] * jnp.dot(pick, rows, preferred_element_type=F32)
        total = part if total is None else total + part
    out_ref[...] = total.astype(BF16)


def add_kernel(slot_ref, r0, r1, r2, r3, out_ref):
    t = slot_ref.shape[0]
    slot = [slot_ref[:, k : k + 1].astype(jnp.int32) for k in range(2)]
    total = None
    for j, ref in enumerate((r0, r1, r2, r3)):
        at = iota((t, 4 * CAP), 1) + j * 4 * CAP
        pick = jnp.where((at == slot[0]) | (at == slot[1]), 1.0, 0.0).astype(BF16)
        part = jnp.dot(pick, ref[...], preferred_element_type=F32)
        total = part if total is None else total + part
    out_ref[...] = total.astype(BF16)


def dot(a, b, ca, cb):
    return lax.dot_general(a, b, (((ca,), (cb,)), ((), ())), preferred_element_type=F32)


def expert_kernel(place, x_ref, c0, c1, c2, c3, *refs):
    blocks, flipped = refs[:8], refs[8:10]
    dsts, res = refs[10:17], refs[17:24]
    w, xs, cs, hid, ga, gb, sems, out_sems = refs[24:]
    o0, o1, o2, o3, cg, mine, other = res
    y, zh, core = place[0], place[1], place[2]
    moves = []

    def move(src, dst):
        moves.append(pltpu.make_async_copy(src, dst, sems.at[len(moves)]))
        moves[-1].start()

    for side in range(2):
        c = lax.rem(core + side, 2)
        block = [blocks[i] if side == 0 else flipped[i // 4].at[i % 4] for i in range(8)]
        for k, (step, h) in enumerate(((0, 0), (0, 1), (3, 0), (1, 0), (3, 1), (1, 1))):
            at = ((lax.rem(y + step, 4) * 2 + lax.rem(zh + h, 2)) * 2 + c) * 64
            move(block[k], w.at[:, pl.ds(pl.multiple_of(at, 64), 64), :])
        for h in range(2):
            at = ((lax.rem(y + 2, 4) * 2 + lax.rem(zh + h, 2)) * 2 + c) * 64
            for q in range(2):
                to = pl.multiple_of(at + 32 * q, 32)
                move(block[6 + q].at[:, 32 * h : 32 * h + 32, :], w.at[:, pl.ds(to, 32), :])
    for j, c in enumerate((c0, c1, c2, c3)):
        for s in range(4):
            at = (j * 4 + s) * CAP
            move(x_ref.at[s, j], xs.at[pl.ds(at, CAP), :])
            move(c.at[s], cs.at[pl.ds(at, CAP), :])
    for one in moves:
        one.wait()
    sent = [pltpu.make_async_copy(a, b, out_sems.at[i]) for i, (a, b) in enumerate(zip(res, dsts))]

    def first(n, _):
        cols = pl.ds(pl.multiple_of(n * 256, 256), 256)
        for r in range(3):
            rows = slice(r * 256, r * 256 + 256)
            pre_gate = dot(xs[rows], w[0, :, cols], 1, 0)
            pre_up = dot(xs[rows], w[1, :, cols], 1, 0)
            grad_h = dot(cs[rows], w[2, cols, :], 1, 1)
            sig = jax.nn.sigmoid(pre_gate)
            act = pre_gate * sig
            hid[rows, cols] = (act * pre_up).astype(BF16)
            ga[rows, cols] = (grad_h * pre_up * sig * (1.0 + pre_gate * (1.0 - sig))).astype(BF16)
            gb[rows, cols] = (grad_h * act).astype(BF16)
        return 0

    lax.fori_loop(0, 4, first, 0)

    def weight_grads(n, _):
        cols = pl.ds(pl.multiple_of(n * 256, 256), 256)
        rel = lax.rem(n + 4 - y, 4)
        for m, (left, right) in enumerate(((xs, ga), (xs, gb), (hid, cs))):
            part = dot(left[:, cols], right[...], 0, 0).astype(BF16)
            for h in range(2):
                p0, p1 = part[h * 128 : h * 128 + 64], part[h * 128 + 64 : h * 128 + 128]
                mine[rel, m, h] = jnp.where(core == 0, p0, p1)
                other[rel, m, h] = jnp.where(core == 0, p1, p0)
        return 0

    lax.fori_loop(0, 4, weight_grads, 0)
    sent[6].start()
    sent[5].start()

    def returns(n, _):
        cols = pl.ds(pl.multiple_of(n * 256, 256), 256)
        for j, o in enumerate((o0, o1, o2, o3)):
            rows = slice(j * 4 * CAP, (j + 1) * 4 * CAP)
            out = dot(hid[rows], w[2, :, cols], 1, 0).astype(BF16)
            back = (dot(ga[rows], w[0, cols, :], 1, 1) + dot(gb[rows], w[1, cols, :], 1, 1)).astype(BF16)
            for s in range(4):
                o[s, :, cols] = out[s * CAP : (s + 1) * CAP]
                cg[s, j, :, cols] = back[s * CAP : (s + 1) * CAP]
        return 0

    lax.fori_loop(0, 4, returns, 0)
    for one in sent[:5]:
        one.start()
    for one in sent:
        one.wait()


def plus(a, b):
    return a.astype(F32) + b.astype(F32)


def far_kernel(mine, came, to_r, to_l):
    to_r[...] = plus(mine[:, :, 0:32], came[:, :, 0:32]).astype(BF16)
    to_l[...] = plus(mine[:, :, 32:64], came[:, :, 32:64]).astype(BF16)


def side_kernel(mine, came, fr, fl, to_r, to_l):
    lo, hi = slice(0, 32), slice(32, 64)
    to_r[:, :, lo] = (plus(mine[1, :, :, lo], came[1, :, :, lo]) + fr[...].astype(F32)).astype(BF16)
    to_r[:, :, hi] = plus(mine[1, :, :, hi], came[1, :, :, hi]).astype(BF16)
    to_l[:, :, lo] = plus(mine[3, :, :, lo], came[3, :, :, lo]).astype(BF16)
    to_l[:, :, hi] = (plus(mine[3, :, :, hi], came[3, :, :, hi]) + fl[...].astype(F32)).astype(BF16)


def here_kernel(place, mine, came, fr, fl, away, here):
    zh = place[1]
    for z, out in ((zh, here), (1 - zh, away)):
        total = plus(mine[:, z], came[:, z]) + plus(fr[:, z], fl[:, z])
        out[...] = total.astype(out.dtype)


def last_kernel(here, came, a, b, c):
    for m, out in enumerate((a, b, c)):
        out[0] = here[m] + came[m].astype(F32)


def shards(tokens, route_ids, gate_values, w_gate, w_up, w_down, swap_flags, out_grad):
    xi, zl = lax.axis_index("x"), lax.axis_index("z_lo")
    yi, zh, core = lax.axis_index("y"), lax.axis_index("z_hi"), lax.axis_index("core")
    t, d = tokens.shape
    own = xi * 4 + zl
    moved = swap_flags[own % 8] != swap_flags[own % 8 + 8]
    place = jnp.stack([yi, zh, core, zl]).astype(jnp.int32)
    flags = swap_flags.astype(jnp.int32)
    piece = shape(4, CAP, d)

    w_own = copies((w_gate[0], w_up[0], w_down[0]), [shape(3, 64, d)], [(m, ALL, 0, m) for m in range(3)])[0]
    w = jnp.where(moved, x_swap(w_own), w_own)
    *sent_x, sent_c, slot = staged(
        prep_kernel,
        (piece, piece, piece, piece, shape(4, 4, CAP, d), shape(t, 8, dtype=F32)),
        (route_ids.T, gate_values.T, tokens, out_grad),
        smem=(flags,),
        flops=4 * 16 * CAP * t * d,
    )
    w, sent_x, sent_c = lax.optimization_barrier((w, sent_x, sent_c))
    w2 = flip(w, "z_hi")
    r0, l0 = y_move(w, 1), y_move(w, 3)

    came_x = [z_move(sent_x[j], j) for j in range(4)]
    came_c = x_exchange(sent_c)
    w2, r0, l0, came_x, came_c = lax.optimization_barrier((w2, r0, l0, came_x, came_c))

    r1, l1 = y_move(w2, 1), y_move(w2, 3)
    recv_x = x_exchange(join_classes(came_x))
    recv_c = [z_move(a, j) for j, a in enumerate(split_classes(came_c))]
    half = shape(3, 64, d)
    lo, hi = (ALL, slice(0, 32)), (ALL, slice(32, 64))
    early = flip(stack((w, w2, r0, l0)), "core")
    to_r, to_l = copies(
        (r0, r1, l0, l1),
        [half, half],
        [(0, lo, 0, lo), (1, lo, 0, hi), (2, hi, 1, lo), (3, hi, 1, hi)],
    )
    fr, fl = y_move(to_r, 1), y_move(to_l, 3)
    fr, fl, recv_x, recv_c = lax.optimization_barrier((fr, fl, recv_x, recv_c))
    late = flip(stack((r1, l1, fr, fl)), "core")

    bf = lambda *dims: pltpu.VMEM(dims, BF16)
    outs = (piece, piece, piece, piece, shape(4, 4, CAP, d), shape(4, 3, 2, 64, d), shape(4, 3, 2, 64, d))
    *out, copy_grad, mine, other = pl.pallas_call(
        expert_kernel,
        out_shape=outs,
        in_specs=[SMEM] + [HBM] * 15,
        out_specs=tuple(HBM for _ in outs),
        scratch_shapes=[bf(*o.shape) for o in outs]
        + [bf(3, d, d)]
        + [bf(16 * CAP, d) for _ in range(5)]
        + [pltpu.SemaphoreType.DMA((52,)), pltpu.SemaphoreType.DMA((7,))],
        compiler_params=pltpu.CompilerParams(vmem_limit_bytes=60 * 2**20),
        cost_estimate=pl.CostEstimate(
            flops=18 * 16 * CAP * d * d, bytes_accessed=20 * 2**20, transcendentals=0
        ),
    )(place, recv_x, *recv_c, w, w2, r0, l0, r1, l1, fr, fl, early, late)

    out = [z_move(out[j], j, True) for j in range(4)]
    ret = x_exchange(copy_grad)
    came = flip(other, "core")
    piece3, row3 = shape(3, 2, 64, d), shape(3, 2, 32, d)
    to_r, to_l = staged(far_kernel, (row3, row3), ((mine, 2), (came, 2)))
    fr, fl = y_move(to_r, 1), y_move(to_l, 3)
    fr, fl, out = lax.optimization_barrier((fr, fl, out))
    to_r, to_l = staged(side_kernel, (piece3, piece3), (mine, came, fr, fl))
    fr, fl = y_move(to_r, 1), y_move(to_l, 3)
    ret = [z_move(a, j, True) for j, a in enumerate(split_classes(ret))]
    back = x_exchange(join_classes(out)).reshape(-1, d)
    fr, fl, ret[1], ret[3] = lax.optimization_barrier((fr, fl, ret[1], ret[3]))
    away, here = staged(
        here_kernel, (shape(3, 64, d), shape(3, 64, d, dtype=F32)), ((mine, 0), (came, 0), fr, fl), smem=(place,)
    )
    came = flip(away, "z_hi")
    (layer_out,) = staged(mix_kernel, (shape(t, d),), (slot, back), flops=4 * 16 * CAP * t * d)
    ret = [r.reshape(-1, d) for r in ret]
    (grad_tokens,) = staged(add_kernel, (shape(t, d),), (slot, *ret), flops=2 * 16 * CAP * t * d)
    one = shape(1, 64, d, dtype=F32)
    grads = staged(last_kernel, (one, one, one), (here, came))
    return layer_out, grad_tokens, *grads


def solution(mesh):
    fine = Mesh(mesh.devices.reshape(SIZES), AXES)
    rows = P(AXES, None)
    weight = P(("x", "z_lo"), ("y", "z_hi", "core"), None)
    return jax.shard_map(
        shards,
        mesh=fine,
        in_specs=(rows, rows, rows, weight, weight, weight, P(), rows),
        out_specs=(rows, rows, weight, weight, weight),
        check_vma=False,
    )
```

```python
import jax
import jax.numpy as jnp
from jax import lax
from jax.experimental import pallas as pl
from jax.experimental.pallas import tpu as pltpu
from jax.sharding import Mesh, PartitionSpec as P

AXES = ("x", "z_lo", "y", "z_hi", "core")
SIZES = (4, 4, 4, 2, 2)
CAP = 48
BF16 = jnp.bfloat16
F32 = jnp.float32
HBM = pl.BlockSpec(memory_space=pltpu.HBM)
SMEM = pl.BlockSpec(memory_space=pltpu.SMEM)


def flat(x, zl, y, zh, c):
    return (((x * 4 + zl) * 4 + y) * 2 + zh) * 2 + c


def z_pairs(j, back):
    pairs = []
    for x in range(4):
        for zl in range(4):
            for y in range(4):
                for zh in range(2):
                    for c in range(2):
                        step = (0, 1, 2 if c == 0 else -2, -1)[j]
                        z = (zh * 4 + zl + step) % 8
                        here, there = flat(x, zl, y, zh, c), flat(x, z % 4, y, z // 4, c)
                        pairs.append((there, here) if back else (here, there))
    return pairs


def z_move(a, j, back=False):
    return a if j == 0 else lax.ppermute(a, AXES, z_pairs(j, back))


def y_move(a, step):
    return lax.ppermute(a, "y", [(i, (i + step) % 4) for i in range(4)])


def x_swap(a):
    return lax.ppermute(a, "x", [(i, i ^ 2) for i in range(4)])


def x_exchange(a):
    return lax.all_to_all(a, "x", split_axis=0, concat_axis=0, tiled=True)


def flip(a, axis):
    return lax.ppermute(a, axis, [(0, 1), (1, 0)])


def iota(shape, dim):
    return lax.broadcasted_iota(jnp.int32, shape, dim)


def shape(*dims, dtype=BF16):
    return jax.ShapeDtypeStruct(dims, dtype)


def staged(body, outs, arrays, smem=(), scratch=(), flops=0):
    k, n, m = len(smem), len(arrays), len(outs)
    part = [a[1] if isinstance(a, tuple) else None for a in arrays]
    arrays = [a[0] if isinstance(a, tuple) else a for a in arrays]

    def kernel(*refs):
        smems, srcs, dsts = refs[:k], refs[k : k + n], refs[k + n : k + n + m]
        ins, res = refs[k + n + m : k + 2 * n + m], refs[k + 2 * n + m : k + 2 * n + 2 * m]
        sems, rest = refs[-1], refs[k + 2 * n + 2 * m : -1]
        srcs = [a if i is None else a.at[i] for a, i in zip(srcs, part)]
        moves = [pltpu.make_async_copy(a, b, sems.at[i]) for i, (a, b) in enumerate(zip(srcs, ins))]
        for one in moves:
            one.start()
        for one in moves:
            one.wait()
        body(*smems, *ins, *res, *rest)
        moves = [pltpu.make_async_copy(a, b, sems.at[n + i]) for i, (a, b) in enumerate(zip(res, dsts))]
        for one in moves:
            one.start()
        for one in moves:
            one.wait()

    return pl.pallas_call(
        kernel,
        out_shape=tuple(outs),
        in_specs=[SMEM] * k + [HBM] * n,
        out_specs=tuple(HBM for _ in outs),
        scratch_shapes=[
            pltpu.VMEM(a.shape if i is None else a.shape[1:], a.dtype) for a, i in zip(arrays, part)
        ]
        + [pltpu.VMEM(o.shape, o.dtype) for o in outs]
        + list(scratch)
        + [pltpu.SemaphoreType.DMA((n + m,))],
        compiler_params=pltpu.CompilerParams(vmem_limit_bytes=60 * 2**20),
        cost_estimate=pl.CostEstimate(flops=flops, bytes_accessed=4 * 2**20, transcendentals=0),
    )(*smem, *arrays)


def copies(arrays, outs, pieces):
    n, m = len(arrays), len(outs)

    def kernel(*refs):
        srcs, dsts, mids, sems = refs[:n], refs[n : n + m], refs[n + m : n + 2 * m], refs[-1]
        moves = [
            pltpu.make_async_copy(srcs[i].at[at], mids[o].at[to], sems.at[p])
            for p, (i, at, o, to) in enumerate(pieces)
        ]
        for one in moves:
            one.start()
        for one in moves:
            one.wait()
        moves = [
            pltpu.make_async_copy(a, b, sems.at[len(pieces) + o]) for o, (a, b) in enumerate(zip(mids, dsts))
        ]
        for one in moves:
            one.start()
        for one in moves:
            one.wait()

    return pl.pallas_call(
        kernel,
        out_shape=tuple(outs),
        in_specs=[HBM] * n,
        out_specs=tuple(HBM for _ in outs),
        scratch_shapes=[pltpu.VMEM(o.shape, o.dtype) for o in outs]
        + [pltpu.SemaphoreType.DMA((len(pieces) + m,))],
        compiler_params=pltpu.CompilerParams(vmem_limit_bytes=60 * 2**20),
        cost_estimate=pl.CostEstimate(flops=0, bytes_accessed=4 * 2**20, transcendentals=0),
    )(*arrays)


ALL = slice(None)


def stack(arrays):
    return copies(
        arrays, [shape(len(arrays), *arrays[0].shape)], [(i, ALL, 0, i) for i in range(len(arrays))]
    )[0]


def join_classes(arrays):
    d = arrays[0].shape[-1]
    return copies(arrays, [shape(4, 4, CAP, d)], [(j, ALL, 0, (ALL, j)) for j in range(4)])[0]


def split_classes(a):
    d = a.shape[-1]
    return copies((a,), [shape(4, CAP, d)] * 4, [(0, (ALL, j), j, ALL) for j in range(4)])


def prep_kernel(flags, ids_ref, gate_ref, tok_ref, grad_ref, x0, x1, x2, x3, c_ref, slot_ref):
    t = ids_ref.shape[1]
    zl = lax.axis_index("z_lo")
    ids = ids_ref[...]
    shift = jnp.zeros_like(ids)
    for p in range(8):
        step = jnp.where(flags[p] != flags[p + 8], 8, 0)
        shift = shift + jnp.where((ids & 7) == p, step, 0)
    holder = (ids + shift) & 15
    hx, hj = holder >> 2, ((holder & 3) - zl) & 3
    lab = hj * 4 + hx
    hot = [lab[k : k + 1, :] == iota((16, t), 0) for k in range(2)]
    both = jnp.where(hot[0] | hot[1], 1.0, 0.0).astype(BF16)
    earlier = jnp.where(iota((t, t), 0) < iota((t, t), 1), 1.0, 0.0).astype(BF16)
    count = jnp.dot(both, earlier, preferred_element_type=F32)
    diagonal = iota((t, t), 0) == iota((t, t), 1)
    gate = gate_ref[...]
    slot, weight = [], []
    for k in range(2):
        rank = jnp.sum(jnp.where(hot[k], count, 0.0), axis=0, keepdims=True).astype(jnp.int32)
        one, two = lab[k : k + 1, :] * CAP + rank, (hx[k : k + 1, :] * 4 + hj[k : k + 1, :]) * CAP + rank
        slot.append(one)
        weight.append(gate[k : k + 1, :])
        for at, row in ((k, one.astype(F32)), (k + 2, two.astype(F32)), (k + 4, weight[k])):
            slot_ref[:, at : at + 1] = jnp.sum(jnp.where(diagonal, row, 0.0), axis=1, keepdims=True)
    tok = tok_ref[...]
    grad = grad_ref[...]
    for j, out in enumerate((x0, x1, x2, x3)):
        rows = iota((4 * CAP, t), 0) + j * 4 * CAP
        m0, m1 = rows == slot[0], rows == slot[1]
        pick = jnp.where(m0 | m1, 1.0, 0.0).astype(BF16)
        scale = jnp.sum(
            jnp.where(m0, weight[0], 0.0) + jnp.where(m1, weight[1], 0.0), axis=1, keepdims=True
        )
        xr = jnp.dot(pick, tok, preferred_element_type=F32).astype(BF16)
        cr = (scale * jnp.dot(pick, grad, preferred_element_type=F32)).astype(BF16)
        for e in range(4):
            out[e] = xr[e * CAP : (e + 1) * CAP]
            c_ref[e, j] = cr[e * CAP : (e + 1) * CAP]


def mix_kernel(slot_ref, rows_ref, out_ref):
    t, s = slot_ref.shape[0], rows_ref.shape[0]
    rows = rows_ref[...]
    total = None
    for k in range(2):
        slot = slot_ref[:, k + 2 : k + 3].astype(jnp.int32)
        pick = jnp.where(iota((t, s), 1) == slot, 1.0, 0.0).astype(BF16)
        part = slot_ref[:, k + 4 : k + 5] * jnp.dot(pick, rows, preferred_element_type=F32)
        total = part if total is None else total + part
    out_ref[...] = total.astype(BF16)


def add_kernel(slot_ref, r0, r1, r2, r3, out_ref):
    t = slot_ref.shape[0]
    slot = [slot_ref[:, k : k + 1].astype(jnp.int32) for k in range(2)]
    total = None
    for j, ref in enumerate((r0, r1, r2, r3)):
        at = iota((t, 4 * CAP), 1) + j * 4 * CAP
        pick = jnp.where((at == slot[0]) | (at == slot[1]), 1.0, 0.0).astype(BF16)
        part = jnp.dot(pick, ref[...], preferred_element_type=F32)
        total = part if total is None else total + part
    out_ref[...] = total.astype(BF16)


def dot(a, b, ca, cb):
    return lax.dot_general(a, b, (((ca,), (cb,)), ((), ())), preferred_element_type=F32)


def expert_kernel(place, x_ref, c0, c1, c2, c3, *refs):
    blocks, flipped = refs[:8], refs[8:10]
    dsts, res = refs[10:17], refs[17:24]
    w, xs, cs, hid, ga, gb, sems, out_sems = refs[24:]
    o0, o1, o2, o3, cg, mine, other = res
    y, zh, core = place[0], place[1], place[2]
    moves = []

    def move(src, dst):
        moves.append(pltpu.make_async_copy(src, dst, sems.at[len(moves)]))
        moves[-1].start()

    for side in range(2):
        c = lax.rem(core + side, 2)
        block = [blocks[i] if side == 0 else flipped[i // 4].at[i % 4] for i in range(8)]
        for k, (step, h) in enumerate(((0, 0), (0, 1), (3, 0), (1, 0), (3, 1), (1, 1))):
            at = ((lax.rem(y + step, 4) * 2 + lax.rem(zh + h, 2)) * 2 + c) * 64
            move(block[k], w.at[:, pl.ds(pl.multiple_of(at, 64), 64), :])
        for h in range(2):
            at = ((lax.rem(y + 2, 4) * 2 + lax.rem(zh + h, 2)) * 2 + c) * 64
            for q in range(2):
                to = pl.multiple_of(at + 32 * q, 32)
                move(block[6 + q].at[:, 32 * h : 32 * h + 32, :], w.at[:, pl.ds(to, 32), :])
    for j, c in enumerate((c0, c1, c2, c3)):
        for s in range(4):
            at = (j * 4 + s) * CAP
            move(x_ref.at[s, j], xs.at[pl.ds(at, CAP), :])
            move(c.at[s], cs.at[pl.ds(at, CAP), :])
    for one in moves:
        one.wait()
    sent = [pltpu.make_async_copy(a, b, out_sems.at[i]) for i, (a, b) in enumerate(zip(res, dsts))]

    def first(n, _):
        cols = pl.ds(pl.multiple_of(n * 256, 256), 256)
        for r in range(2):
            rows = slice(r * 384, r * 384 + 384)
            pre_gate = dot(xs[rows], w[0, :, cols], 1, 0)
            pre_up = dot(xs[rows], w[1, :, cols], 1, 0)
            grad_h = dot(cs[rows], w[2, cols, :], 1, 1)
            sig = jax.nn.sigmoid(pre_gate)
            act = pre_gate * sig
            hid[rows, cols] = (act * pre_up).astype(BF16)
            ga[rows, cols] = (grad_h * pre_up * sig * (1.0 + pre_gate * (1.0 - sig))).astype(BF16)
            gb[rows, cols] = (grad_h * act).astype(BF16)
        return 0

    lax.fori_loop(0, 4, first, 0)

    def weight_grads(n, _):
        cols = pl.ds(pl.multiple_of(n * 256, 256), 256)
        rel = lax.rem(n + 4 - y, 4)
        for m, (left, right) in enumerate(((xs, ga), (xs, gb), (hid, cs))):
            part = dot(left[:, cols], right[...], 0, 0).astype(BF16)
            for h in range(2):
                p0, p1 = part[h * 128 : h * 128 + 64], part[h * 128 + 64 : h * 128 + 128]
                mine[rel, m, h] = jnp.where(core == 0, p0, p1)
                other[rel, m, h] = jnp.where(core == 0, p1, p0)
        return 0

    lax.fori_loop(0, 4, weight_grads, 0)
    sent[6].start()
    sent[5].start()

    def returns(n, _):
        cols = pl.ds(pl.multiple_of(n * 256, 256), 256)
        out = dot(hid[...], w[2, :, cols], 1, 0).astype(BF16)
        back = (dot(ga[...], w[0, cols, :], 1, 1) + dot(gb[...], w[1, cols, :], 1, 1)).astype(BF16)
        for j, o in enumerate((o0, o1, o2, o3)):
            for s in range(4):
                at = (j * 4 + s) * CAP
                o[s, :, cols] = out[at : at + CAP]
                cg[s, j, :, cols] = back[at : at + CAP]
        return 0

    lax.fori_loop(0, 4, returns, 0)
    for one in sent[:5]:
        one.start()
    for one in sent:
        one.wait()


def plus(a, b):
    return a.astype(F32) + b.astype(F32)


def far_kernel(mine, came, to_r, to_l):
    to_r[...] = plus(mine[:, :, 0:32], came[:, :, 0:32]).astype(BF16)
    to_l[...] = plus(mine[:, :, 32:64], came[:, :, 32:64]).astype(BF16)


def side_kernel(mine, came, fr, fl, to_r, to_l):
    lo, hi = slice(0, 32), slice(32, 64)
    to_r[:, :, lo] = (plus(mine[1, :, :, lo], came[1, :, :, lo]) + fr[...].astype(F32)).astype(BF16)
    to_r[:, :, hi] = plus(mine[1, :, :, hi], came[1, :, :, hi]).astype(BF16)
    to_l[:, :, lo] = plus(mine[3, :, :, lo], came[3, :, :, lo]).astype(BF16)
    to_l[:, :, hi] = (plus(mine[3, :, :, hi], came[3, :, :, hi]) + fl[...].astype(F32)).astype(BF16)


def here_kernel(place, mine, came, fr, fl, away, here):
    zh = place[1]
    for z, out in ((zh, here), (1 - zh, away)):
        total = plus(mine[:, z], came[:, z]) + plus(fr[:, z], fl[:, z])
        out[...] = total.astype(out.dtype)


def last_kernel(here, came, a, b, c):
    for m, out in enumerate((a, b, c)):
        out[0] = here[m] + came[m].astype(F32)


def shards(tokens, route_ids, gate_values, w_gate, w_up, w_down, swap_flags, out_grad):
    xi, zl = lax.axis_index("x"), lax.axis_index("z_lo")
    yi, zh, core = lax.axis_index("y"), lax.axis_index("z_hi"), lax.axis_index("core")
    t, d = tokens.shape
    own = xi * 4 + zl
    moved = swap_flags[own % 8] != swap_flags[own % 8 + 8]
    place = jnp.stack([yi, zh, core, zl]).astype(jnp.int32)
    flags = swap_flags.astype(jnp.int32)
    piece = shape(4, CAP, d)

    w_own = copies((w_gate[0], w_up[0], w_down[0]), [shape(3, 64, d)], [(m, ALL, 0, m) for m in range(3)])[0]
    w = jnp.where(moved, x_swap(w_own), w_own)
    *sent_x, sent_c, slot = staged(
        prep_kernel,
        (piece, piece, piece, piece, shape(4, 4, CAP, d), shape(t, 8, dtype=F32)),
        (route_ids.T, gate_values.T, tokens, out_grad),
        smem=(flags,),
        flops=4 * 16 * CAP * t * d,
    )
    w, sent_x, sent_c = lax.optimization_barrier((w, sent_x, sent_c))
    w2 = flip(w, "z_hi")
    r0, l0 = y_move(w, 1), y_move(w, 3)

    came_x = [z_move(sent_x[j], j) for j in range(4)]
    came_c = x_exchange(sent_c)
    w2, r0, l0, came_x, came_c = lax.optimization_barrier((w2, r0, l0, came_x, came_c))

    r1, l1 = y_move(w2, 1), y_move(w2, 3)
    recv_x = x_exchange(join_classes(came_x))
    recv_c = [z_move(a, j) for j, a in enumerate(split_classes(came_c))]
    half = shape(3, 64, d)
    lo, hi = (ALL, slice(0, 32)), (ALL, slice(32, 64))
    early = flip(stack((w, w2, r0, l0)), "core")
    to_r, to_l = copies(
        (r0, r1, l0, l1),
        [half, half],
        [(0, lo, 0, lo), (1, lo, 0, hi), (2, hi, 1, lo), (3, hi, 1, hi)],
    )
    fr, fl = y_move(to_r, 1), y_move(to_l, 3)
    fr, fl, recv_x, recv_c = lax.optimization_barrier((fr, fl, recv_x, recv_c))
    late = flip(stack((r1, l1, fr, fl)), "core")

    bf = lambda *dims: pltpu.VMEM(dims, BF16)
    outs = (piece, piece, piece, piece, shape(4, 4, CAP, d), shape(4, 3, 2, 64, d), shape(4, 3, 2, 64, d))
    *out, copy_grad, mine, other = pl.pallas_call(
        expert_kernel,
        out_shape=outs,
        in_specs=[SMEM] + [HBM] * 15,
        out_specs=tuple(HBM for _ in outs),
        scratch_shapes=[bf(*o.shape) for o in outs]
        + [bf(3, d, d)]
        + [bf(16 * CAP, d) for _ in range(5)]
        + [pltpu.SemaphoreType.DMA((52,)), pltpu.SemaphoreType.DMA((7,))],
        compiler_params=pltpu.CompilerParams(vmem_limit_bytes=60 * 2**20),
        cost_estimate=pl.CostEstimate(
            flops=18 * 16 * CAP * d * d, bytes_accessed=20 * 2**20, transcendentals=0
        ),
    )(place, recv_x, *recv_c, w, w2, r0, l0, r1, l1, fr, fl, early, late)

    out = [z_move(out[j], j, True) for j in range(4)]
    ret = x_exchange(copy_grad)
    came = flip(other, "core")
    piece3, row3 = shape(3, 2, 64, d), shape(3, 2, 32, d)
    to_r, to_l = staged(far_kernel, (row3, row3), ((mine, 2), (came, 2)))
    fr, fl = y_move(to_r, 1), y_move(to_l, 3)
    fr, fl, out = lax.optimization_barrier((fr, fl, out))
    to_r, to_l = staged(side_kernel, (piece3, piece3), (mine, came, fr, fl))
    fr, fl = y_move(to_r, 1), y_move(to_l, 3)
    ret = [z_move(a, j, True) for j, a in enumerate(split_classes(ret))]
    back = x_exchange(join_classes(out)).reshape(-1, d)
    fr, fl, ret[1], ret[3] = lax.optimization_barrier((fr, fl, ret[1], ret[3]))
    away, here = staged(
        here_kernel, (shape(3, 64, d), shape(3, 64, d, dtype=F32)), ((mine, 0), (came, 0), fr, fl), smem=(place,)
    )
    came = flip(away, "z_hi")
    (layer_out,) = staged(mix_kernel, (shape(t, d),), (slot, back), flops=4 * 16 * CAP * t * d)
    ret = [r.reshape(-1, d) for r in ret]
    (grad_tokens,) = staged(add_kernel, (shape(t, d),), (slot, *ret), flops=2 * 16 * CAP * t * d)
    one = shape(1, 64, d, dtype=F32)
    grads = staged(last_kernel, (one, one, one), (here, came))
    return layer_out, grad_tokens, *grads


def solution(mesh):
    fine = Mesh(mesh.devices.reshape(SIZES), AXES)
    rows = P(AXES, None)
    weight = P(("x", "z_lo"), ("y", "z_hi", "core"), None)
    return jax.shard_map(
        shards,
        mesh=fine,
        in_specs=(rows, rows, rows, weight, weight, weight, P(), rows),
        out_specs=(rows, rows, weight, weight, weight),
        check_vma=False,
    )
```
